512 devices in a mesh: grp: 64 (over z, x), mem: 8 (over y, core).
Axes of the slice: x: 4, y: 4, z: 16, core: 2. Of those that a mesh axis runs over, the one named last changes fastest.
Arguments:
- embeddings: bfloat16 [64, 32, 64, 768], P('grp', 'mem'), may hold values from -30 to 30
- counts: int32 [64, 64], replicated, may hold values from 0 to 32, as said below
Outputs:
- nearest: float32 [64, 32, 64], P('grp', 'mem')
The draws below stay inside these ranges and needn't reach their ends.
Inputs may be any that keep to these rules, and one draw needn't show every extreme that they name: counts[s, c] slots of source group s for cluster c are filled, the first ones; some entry equals 32 and some equals 0.
All inputs are finite; a program needn't handle non-finite values.
Results may differ from the reference program's by a relative error of at most 0.00067.
Values may be sent and summed in bfloat16 or wider, within the bound.
No kernel may reach another device: no remote copies, remote signals or barrier semaphores. Data moves between devices by JAX's collectives and lax.ppermute only.
A program may use at most 64 MiB of HBM per device.

```python
import jax
import jax.numpy as jnp
from jax import lax

D = 768
SLOT = 32
CLUSTERS = 64


def draw_counts(key, part):
    key = jax.random.fold_in(key, 11)
    first, second, third, fourth = jax.random.split(key, 4)
    level = jax.random.randint(first, (1, CLUSTERS), 1, 5)
    raw = jax.random.randint(second, (CLUSTERS, CLUSTERS), 0, SLOT + 1)
    filled = jnp.minimum(SLOT, raw * (level + 2) // 4)
    spot_full = jax.random.randint(third, (2,), 0, CLUSTERS)
    spot_empty = jax.random.randint(fourth, (2,), 0, CLUSTERS)
    filled = filled.at[spot_empty[0], spot_empty[1]].set(0)
    filled = filled.at[spot_full[0], spot_full[1]].set(SLOT)
    return filled.astype(jnp.int32)


def draw_embeddings(key, part):
    key = jax.random.fold_in(key, 23)
    first, second, third, fourth = jax.random.split(key, 4)
    sources = max(CLUSTERS * SLOT // 4, 1)
    protos = jax.random.normal(first, (CLUSTERS, sources, D), jnp.float32)
    picks = jax.random.randint(second, (CLUSTERS, SLOT, CLUSTERS), 0, sources)
    owner = jnp.arange(CLUSTERS, dtype=jnp.int32)[None, None, :]
    base = protos[owner, picks]
    weight = jax.random.uniform(third, (CLUSTERS, SLOT, CLUSTERS, 1), jnp.float32, 0.35, 1.2)
    noise = jax.random.normal(fourth, (CLUSTERS, SLOT, CLUSTERS, D), jnp.float32)
    values = jnp.clip(base + weight * noise, -30.0, 30.0)
    return values.astype(jnp.bfloat16)


def setup_inputs(seed: int = 0) -> dict:
    splits = jax.random.split(jax.random.key(seed), 3)
    embeddings = draw_embeddings(jax.random.fold_in(splits[2], 71), 0)
    counts = draw_counts(jax.random.fold_in(splits[2], 71), 0)
    return {"embeddings": embeddings, "counts": counts}


EPS = 1e-06

def reference(embeddings, counts):
    values = embeddings.astype(jnp.float32)
    units = (values * lax.rsqrt(lax.optimization_barrier(jnp.sum(values * values, axis=-1, keepdims=True)) + EPS)).astype(jnp.bfloat16)
    groups = units.shape[0]
    slots = units.shape[1]
    total = groups * slots
    block = 512 if total % 512 == 0 else total
    position = jnp.arange(total, dtype=jnp.int32)

    def one_cluster(cluster):
        rows = lax.dynamic_index_in_dim(units, cluster, 2, keepdims=False)
        rows = jnp.transpose(rows, (1, 0, 2)).reshape(total, units.shape[3])
        sizes = lax.dynamic_index_in_dim(counts, cluster, 1, keepdims=False)
        filled = (jnp.arange(slots, dtype=jnp.int32)[:, None] < sizes[None, :]).reshape(total)

        def one_block(start):
            part = lax.dynamic_slice_in_dim(rows, start, block, 0)
            scores = jnp.dot(part, rows.T, preferred_element_type=jnp.float32)
            here = start + jnp.arange(block, dtype=jnp.int32)
            allowed = filled[None, :] & (position[None, :] < here[:, None])
            return lax.optimization_barrier(jnp.max(jnp.where(allowed, scores, jnp.float32(-1.0)), axis=1))
        starts = jnp.arange(0, total, block, dtype=jnp.int32)
        best = lax.map(one_block, starts).reshape(total)
        return jnp.transpose(best.reshape(slots, groups), (1, 0))
    clusters = jnp.arange(groups, dtype=jnp.int32)
    result = lax.map(one_cluster, clusters)
    return jnp.transpose(result, (1, 2, 0))
```

```python
import jax
import jax.numpy as jnp
from jax import lax
from jax.experimental import pallas as pl
from jax.experimental.pallas import tpu as pltpu
from jax.sharding import PartitionSpec as P

EPS = 1e-06
FAR = 1 << 20
CORES = 2


def nearest_kernel(place_ref, counts_ref, own_ref, sib_ref, keys_ref, out_ref):
    cluster, chip, core = place_ref[0], place_ref[1], place_ref[2]
    chips, rows, _ = keys_ref.shape
    groups = counts_ref.shape[0]
    slots = rows // groups
    column = lax.broadcasted_iota(jnp.int32, counts_ref.shape, 1)
    sizes = jnp.sum(jnp.where(column == cluster, counts_ref[...], 0), axis=1, keepdims=True)
    sizes = jnp.concatenate([sizes] * slots, axis=0)
    row = lax.broadcasted_iota(jnp.int32, (rows, 1), 0)
    lane = lax.broadcasted_iota(jnp.int32, (1, rows), 1)
    own_pos = (chip * CORES + core) * rows + lane
    sib_pos = (chip * CORES + 1 - core) * rows + lane
    own_best = jnp.full((1, rows), -1.0, jnp.float32)
    sib_best = jnp.full((1, rows), -1.0, jnp.float32)
    for block in range(chips):
        start = (block * CORES + core) * rows
        slot = (start + row) // groups
        key_pos = jnp.where(slot < sizes, start + row, FAR)
        keys = keys_ref[block]
        for_own = lax.dot_general(
            keys, own_ref[...], (((1,), (1,)), ((), ())), preferred_element_type=jnp.float32
        )
        for_own = jnp.where(key_pos < own_pos, for_own, -1.0)
        own_best = jnp.maximum(own_best, jnp.max(for_own, axis=0, keepdims=True))
        for_sib = lax.dot_general(
            keys, sib_ref[...], (((1,), (1,)), ((), ())), preferred_element_type=jnp.float32
        )
        for_sib = jnp.where(key_pos < sib_pos, for_sib, -1.0)
        sib_best = jnp.maximum(sib_best, jnp.max(for_sib, axis=0, keepdims=True))
    out_ref[0:1, :] = own_best
    out_ref[1:2, :] = sib_best


def nearest_partial(place, counts, own, sib, keys):
    rows, width = own.shape
    chips = keys.shape[0]
    flops = 2 * 2 * chips * rows * rows * width
    moved = 2 * width * rows * (chips + 2)
    vmem = pl.BlockSpec(memory_space=pltpu.VMEM)
    return pl.pallas_call(
        nearest_kernel,
        out_shape=jax.ShapeDtypeStruct((2, rows), jnp.float32),
        in_specs=[pl.BlockSpec(memory_space=pltpu.SMEM), vmem, vmem, vmem, vmem],
        out_specs=vmem,
        compiler_params=pltpu.CompilerParams(vmem_limit_bytes=32 << 20),
        cost_estimate=pl.CostEstimate(flops=flops, bytes_accessed=moved, transcendentals=0),
    )(place, counts, own, sib, keys)


def make_on_device(members):
    chips = members // CORES
    swap = [(m, m ^ 1) for m in range(members)]
    rings = [[chip * CORES + core for chip in range(chips)] for core in range(CORES)]

    def on_device(embeddings, counts):
        cluster = lax.axis_index("grp")
        member = lax.axis_index("mem")
        slot_dev = embeddings.shape[1]
        groups = embeddings.shape[2]
        width = embeddings.shape[3]
        local = embeddings.reshape(slot_dev, groups, width)
        values = local.astype(jnp.float32)
        units = (
            values * lax.rsqrt(jnp.sum(values * values, axis=-1, keepdims=True) + EPS)
        ).astype(jnp.bfloat16)
        owned = lax.all_to_all(units, "grp", split_axis=1, concat_axis=1, tiled=True)
        nrows = slot_dev * groups
        rows = owned.reshape(nrows, width)
        sib = lax.ppermute(rows, "mem", swap)
        copies = jnp.broadcast_to(rows[None], (chips, nrows, width))
        keys = lax.all_to_all(
            copies, "mem", split_axis=0, concat_axis=0, tiled=True, axis_index_groups=rings
        )
        place = jnp.stack([cluster, member // CORES, member % CORES]).astype(jnp.int32)
        best = nearest_partial(place, counts, rows, sib, keys)
        best = jnp.maximum(best[0], lax.ppermute(best[1], "mem", swap))
        back = lax.all_to_all(
            best.reshape(slot_dev, groups), "grp", split_axis=1, concat_axis=1, tiled=True
        )
        return back.reshape(1, slot_dev, groups)

    return on_device


def solution(mesh):
    return jax.shard_map(
        make_on_device(mesh.shape["mem"]),
        mesh=mesh,
        in_specs=(P("grp", "mem", None, None), P()),
        out_specs=P("grp", "mem", None),
        check_vma=False,
    )
```

```python
import jax
import jax.numpy as jnp
from jax import lax
from jax.experimental import pallas as pl
from jax.experimental.pallas import tpu as pltpu
from jax.sharding import PartitionSpec as P

EPS = 1e-06
FAR = 1 << 20
CORE, NEXT, CROSS = 1, 2, 6


def nearest_kernel(place_ref, counts_ref, query_ref, *refs):
    keys_refs, out_ref = refs[:-1], refs[-1]
    cluster, query_member = place_ref[0], place_ref[1]
    rows = query_ref.shape[0]
    groups = counts_ref.shape[0]
    slots = rows // groups
    column = lax.broadcasted_iota(jnp.int32, counts_ref.shape, 1)
    sizes = jnp.sum(jnp.where(column == cluster, counts_ref[...], 0), axis=1, keepdims=True)
    sizes = jnp.concatenate([sizes] * slots, axis=0)
    row = lax.broadcasted_iota(jnp.int32, (rows, 1), 0)
    lane = lax.broadcasted_iota(jnp.int32, (1, rows), 1)
    query_pos = query_member * rows + lane
    best = jnp.full((1, rows), -1.0, jnp.float32)
    for index, keys_ref in enumerate(keys_refs):
        start = place_ref[2 + index] * rows
        slot = (start + row) // groups
        key_pos = jnp.where(slot < sizes, start + row, FAR)
        score = lax.dot_general(
            keys_ref[...], query_ref[...], (((1,), (1,)), ((), ())), preferred_element_type=jnp.float32
        )
        score = jnp.where(key_pos < query_pos, score, -1.0)
        best = jnp.maximum(best, jnp.max(score, axis=0, keepdims=True))
    out_ref[...] = best


def nearest_of(cluster, counts, query, query_member, keys, key_members):
    rows, width = query.shape
    place = jnp.stack([cluster, query_member, *key_members]).astype(jnp.int32)
    flops = 2 * len(keys) * rows * rows * width
    moved = 2 * width * rows * (len(keys) + 1)
    vmem = pl.BlockSpec(memory_space=pltpu.VMEM)
    return pl.pallas_call(
        nearest_kernel,
        out_shape=jax.ShapeDtypeStruct((1, rows), jnp.float32),
        in_specs=[pl.BlockSpec(memory_space=pltpu.SMEM)] + [vmem] * (2 + len(keys)),
        out_specs=vmem,
        compiler_params=pltpu.CompilerParams(vmem_limit_bytes=32 << 20),
        cost_estimate=pl.CostEstimate(flops=flops, bytes_accessed=moved, transcendentals=0),
    )(place, counts, query, *keys)


def make_on_device(members):
    def trade(array, mask):
        return lax.ppermute(array, "mem", [(m, m ^ mask) for m in range(members)])

    def on_device(embeddings, counts):
        cluster = lax.axis_index("grp")
        member = lax.axis_index("mem")
        slot_dev = embeddings.shape[1]
        groups = embeddings.shape[2]
        width = embeddings.shape[3]
        local = embeddings.reshape(slot_dev, groups, width)
        values = local.astype(jnp.float32)
        units = (
            values * lax.rsqrt(jnp.sum(values * values, axis=-1, keepdims=True) + EPS)
        ).astype(jnp.bfloat16)
        owned = lax.all_to_all(units, "grp", split_axis=1, concat_axis=1, tiled=True)
        rows = owned.reshape(slot_dev * groups, width)
        next_rows = trade(rows, NEXT)
        cross_rows = trade(rows, CROSS)
        sib_rows = trade(rows, CORE)
        next_sib_rows = trade(next_rows, CORE)
        keys = (rows, sib_rows, next_rows, next_sib_rows)
        key_members = (member, member ^ CORE, member ^ NEXT, member ^ NEXT ^ CORE)
        cross_best = nearest_of(cluster, counts, cross_rows, member ^ CROSS, keys, key_members)
        from_cross = trade(cross_best, CROSS)
        own_best = nearest_of(cluster, counts, rows, member, keys, key_members)
        best = jnp.maximum(own_best, from_cross)
        back = lax.all_to_all(
            best.reshape(slot_dev, groups), "grp", split_axis=1, concat_axis=1, tiled=True
        )
        return back.reshape(1, slot_dev, groups)

    return on_device


def solution(mesh):
    return jax.shard_map(
        make_on_device(mesh.shape["mem"]),
        mesh=mesh,
        in_specs=(P("grp", "mem", None, None), P()),
        out_specs=P("grp", "mem", None),
        check_vma=False,
    )
```

```python
import jax
import jax.numpy as jnp
from jax import lax
from jax.experimental import pallas as pl
from jax.experimental.pallas import tpu as pltpu
from jax.sharding import PartitionSpec as P

EPS = 1e-06
FAR = 1 << 20
LANES = 128
CORE, NEXT, CROSS = 1, 2, 6


def nearest_kernel(place_ref, counts_ref, own_ref, sib_ref, cross_ref, next_ref, next_sib_ref, out_ref):
    cluster, member = place_ref[0], place_ref[1]
    rows = own_ref.shape[0]
    groups = counts_ref.shape[0]
    slots = rows // groups
    column = lax.broadcasted_iota(jnp.int32, counts_ref.shape, 1)
    sizes = jnp.sum(jnp.where(column == cluster, counts_ref[...], 0), axis=1, keepdims=True)
    sizes = jnp.broadcast_to(sizes.astype(jnp.float32), (groups, LANES))
    sizes = jnp.transpose(sizes)[0:1, :].astype(jnp.int32)
    sizes = jnp.concatenate([sizes] * slots, axis=1)
    lane = lax.broadcasted_iota(jnp.int32, (1, rows), 1)
    row = lax.broadcasted_iota(jnp.int32, (rows, 1), 0)

    keys = []
    for key_ref, mask in ((own_ref, 0), (sib_ref, CORE), (next_ref, NEXT), (next_sib_ref, NEXT ^ CORE)):
        start = (member ^ mask) * rows
        slot = (start + lane) // groups
        keys.append((key_ref, jnp.where(slot < sizes, start + lane, FAR)))
    results = []
    for query_ref, mask in ((own_ref, 0), (cross_ref, CROSS)):
        query_pos = (member ^ mask) * rows + row
        best = jnp.full((rows, LANES), -1.0, jnp.float32)
        for key_ref, key_pos in keys:
            score = lax.dot_general(
                query_ref[...], key_ref[...], (((1,), (1,)), ((), ())), preferred_element_type=jnp.float32
            )
            score = jnp.where(key_pos < query_pos, score, -1.0)
            for first in range(0, rows, LANES):
                best = jnp.maximum(best, score[:, first : first + LANES])
        best = jnp.max(best, axis=1, keepdims=True)
        results.append(
            jnp.concatenate([best[t * groups : (t + 1) * groups] for t in range(slots)], axis=1)
        )
    own_low = member < (member ^ CROSS)
    out_ref[:groups, 0, :] = jnp.where(own_low, results[0], results[1])
    out_ref[groups:, 0, :] = jnp.where(own_low, results[1], results[0])


def nearest_of(place, counts, own, cross, sib, nxt, next_sib):
    rows, width = own.shape
    groups = counts.shape[0]
    vmem = pl.BlockSpec(memory_space=pltpu.VMEM)
    return pl.pallas_call(
        nearest_kernel,
        out_shape=jax.ShapeDtypeStruct((2 * groups, 1, rows // groups), jnp.float32),
        in_specs=[pl.BlockSpec(memory_space=pltpu.SMEM)] + [vmem] * 6,
        out_specs=vmem,
        compiler_params=pltpu.CompilerParams(vmem_limit_bytes=32 << 20),
        cost_estimate=pl.CostEstimate(
            flops=16 * rows * rows * width, bytes_accessed=10 * rows * width, transcendentals=0
        ),
    )(place, counts, own, sib, cross, nxt, next_sib)


def make_on_device(clusters, members):
    def trade(array, mask):
        return lax.ppermute(array, "mem", [(m, m ^ mask) for m in range(members)])

    lows = [m for m in range(members) if m < m ^ CROSS]
    returns = [
        [c * members + m for m in (low, low ^ CROSS) for c in range(clusters)] for low in lows
    ]

    def on_device(embeddings, counts):
        cluster = lax.axis_index("grp")
        member = lax.axis_index("mem")
        slot_dev = embeddings.shape[1]
        groups = embeddings.shape[2]
        width = embeddings.shape[3]
        local = embeddings.reshape(slot_dev, groups, width)
        values = local.astype(jnp.float32)
        units = (
            values * lax.rsqrt(jnp.sum(values * values, axis=-1, keepdims=True) + EPS)
        ).astype(jnp.bfloat16)
        owned = lax.all_to_all(units, "grp", split_axis=1, concat_axis=1, tiled=True)
        rows = owned.reshape(slot_dev * groups, width)
        next_rows = trade(rows, NEXT)
        cross_rows = trade(rows, CROSS)
        sib_rows = trade(rows, CORE)
        next_sib_rows = trade(next_rows, CORE)
        place = jnp.stack([cluster, member]).astype(jnp.int32)
        best = nearest_of(place, counts, rows, cross_rows, sib_rows, next_rows, next_sib_rows)
        back = lax.all_to_all(
            best, ("grp", "mem"), split_axis=0, concat_axis=0, tiled=True, axis_index_groups=returns
        )
        back = jnp.max(back.reshape(2, groups, slot_dev), axis=0)
        return back.T.reshape(1, slot_dev, groups)

    return on_device


def solution(mesh):
    return jax.shard_map(
        make_on_device(mesh.shape["grp"], mesh.shape["mem"]),
        mesh=mesh,
        in_specs=(P("grp", "mem", None, None), P()),
        out_specs=P("grp", "mem", None),
        check_vma=False,
    )
```

```python
import jax
import jax.numpy as jnp
from jax import lax
from jax.experimental import pallas as pl
from jax.experimental.pallas import tpu as pltpu
from jax.sharding import PartitionSpec as P

EPS = 1e-06
FAR = 1 << 20
LANES = 128
CORE, NEXT, CROSS = 1, 6, 2


def nearest_kernel(place_ref, counts_ref, own_ref, chip_ref, cross_ref, next_ref, out_ref):
    cluster, member = place_ref[0], place_ref[1]
    rows = own_ref.shape[0]
    groups = counts_ref.shape[0]
    slots = rows // groups
    column = lax.broadcasted_iota(jnp.int32, counts_ref.shape, 1)
    sizes = jnp.sum(jnp.where(column == cluster, counts_ref[...], 0), axis=1, keepdims=True)
    sizes = jnp.broadcast_to(sizes.astype(jnp.float32), (groups, LANES))
    sizes = jnp.transpose(sizes)[0:1, :].astype(jnp.int32)
    sizes = jnp.concatenate([sizes] * slots, axis=1)
    lane = lax.broadcasted_iota(jnp.int32, (1, rows), 1)
    row = lax.broadcasted_iota(jnp.int32, (rows, 1), 0)

    keys = []
    for keys_ref, first in ((chip_ref, member & ~CORE), (next_ref, (member ^ NEXT) & ~CORE)):
        for core in range(2):
            start = (first + core) * rows
            slot = (start + lane) // groups
            keys.append((keys_ref, core, jnp.where(slot < sizes, start + lane, FAR)))
    results = []
    for query_ref, mask in ((own_ref, 0), (cross_ref, CROSS)):
        query_pos = (member ^ mask) * rows + row
        best = jnp.full((rows, LANES), -1.0, jnp.float32)
        for keys_ref, core, key_pos in keys:
            score = lax.dot_general(
                query_ref[...], keys_ref[core], (((1,), (1,)), ((), ())), preferred_element_type=jnp.float32
            )
            score = jnp.where(key_pos < query_pos, score, -1.0)
            for first in range(0, rows, LANES):
                best = jnp.maximum(best, score[:, first : first + LANES])
        best = jnp.max(best, axis=1, keepdims=True)
        results.append(
            jnp.concatenate([best[t * groups : (t + 1) * groups] for t in range(slots)], axis=1)
        )
    own_low = member < (member ^ CROSS)
    out_ref[:groups, 0, :] = jnp.where(own_low, results[0], results[1])
    out_ref[groups:, 0, :] = jnp.where(own_low, results[1], results[0])


def nearest_of(place, counts, own, chip, cross, nxt):
    rows, width = own.shape
    groups = counts.shape[0]
    vmem = pl.BlockSpec(memory_space=pltpu.VMEM)
    return pl.pallas_call(
        nearest_kernel,
        out_shape=jax.ShapeDtypeStruct((2 * groups, 1, rows // groups), jnp.float32),
        in_specs=[pl.BlockSpec(memory_space=pltpu.SMEM)] + [vmem] * 5,
        out_specs=vmem,
        compiler_params=pltpu.CompilerParams(vmem_limit_bytes=32 << 20),
        cost_estimate=pl.CostEstimate(
            flops=16 * rows * rows * width, bytes_accessed=10 * rows * width, transcendentals=0
        ),
    )(place, counts, own, chip, cross, nxt)


def make_on_device(clusters, members):
    def trade(array, mask):
        return lax.ppermute(array, "mem", [(m, m ^ mask) for m in range(members)])

    def both_cores(array):
        chips = [[m, m ^ CORE] for m in range(0, members, 2)]
        return lax.all_gather(array, "mem", axis=0, axis_index_groups=chips)

    lows = [m for m in range(members) if m < m ^ CROSS]
    returns = [
        [c * members + m for m in (low, low ^ CROSS) for c in range(clusters)] for low in lows
    ]

    def on_device(embeddings, counts):
        cluster = lax.axis_index("grp")
        member = lax.axis_index("mem")
        slot_dev = embeddings.shape[1]
        groups = embeddings.shape[2]
        width = embeddings.shape[3]
        local = embeddings.reshape(slot_dev, groups, width)
        values = local.astype(jnp.float32)
        units = (
            values * lax.rsqrt(jnp.sum(values * values, axis=-1, keepdims=True) + EPS)
        ).astype(jnp.bfloat16)
        owned = lax.all_to_all(units, "grp", split_axis=1, concat_axis=1, tiled=True)
        rows = owned.reshape(slot_dev * groups, width)
        next_rows = trade(rows, NEXT)
        cross_rows = trade(rows, CROSS)
        chip_rows = both_cores(rows)
        next_chip_rows = both_cores(next_rows)
        place = jnp.stack([cluster, member]).astype(jnp.int32)
        best = nearest_of(place, counts, rows, chip_rows, cross_rows, next_chip_rows)
        back = lax.all_to_all(
            best, ("grp", "mem"), split_axis=0, concat_axis=0, tiled=True, axis_index_groups=returns
        )
        back = jnp.max(back.reshape(2, groups, slot_dev), axis=0)
        return back.T.reshape(1, slot_dev, groups)

    return on_device


def solution(mesh):
    return jax.shard_map(
        make_on_device(mesh.shape["grp"], mesh.shape["mem"]),
        mesh=mesh,
        in_specs=(P("grp", "mem", None, None), P()),
        out_specs=P("grp", "mem", None),
        check_vma=False,
    )
```

```python
import jax
import jax.numpy as jnp
from jax import lax
from jax.experimental import pallas as pl
from jax.experimental.pallas import tpu as pltpu
from jax.sharding import PartitionSpec as P

EPS = 1e-06
FAR = 1 << 20
LANES = 128
CORE, NEXT, CROSS = 1, 6, 2
FLIP = 63


def nearest_kernel(place_ref, counts_ref, own_ref, chip_ref, cross_ref, next_ref, out_ref):
    cluster, member = place_ref[0], place_ref[1]
    rows = own_ref.shape[0]
    groups = counts_ref.shape[0]
    slots = rows // groups
    column = lax.broadcasted_iota(jnp.int32, counts_ref.shape, 1)
    sizes = jnp.sum(jnp.where(column == cluster, counts_ref[...], 0), axis=1, keepdims=True)
    source = lax.broadcasted_iota(jnp.int32, (groups, groups), 0)
    place = lax.broadcasted_iota(jnp.int32, (groups, groups), 1)
    sizes = jnp.sum(jnp.where(source == place ^ FLIP, sizes, 0), axis=0, keepdims=True)
    sizes = jnp.concatenate([sizes] * slots, axis=1)
    lane = lax.broadcasted_iota(jnp.int32, (1, rows), 1) ^ FLIP
    row = lax.broadcasted_iota(jnp.int32, (rows, 1), 0) ^ FLIP

    keys = []
    for keys_ref, first in ((chip_ref, member & ~CORE), (next_ref, (member ^ NEXT) & ~CORE)):
        for core in range(2):
            start = (first + core) * rows
            slot = (start + lane) // groups
            keys.append((keys_ref, core, jnp.where(slot < sizes, start + lane, FAR)))
    results = []
    for query_ref, mask in ((own_ref, 0), (cross_ref, CROSS)):
        query_pos = (member ^ mask) * rows + row
        best = jnp.full((rows, LANES), -1.0, jnp.float32)
        for keys_ref, core, key_pos in keys:
            score = lax.dot_general(
                query_ref[...], keys_ref[core], (((1,), (1,)), ((), ())), preferred_element_type=jnp.float32
            )
            score = jnp.where(key_pos < query_pos, score, -1.0)
            for first in range(0, rows, LANES):
                best = jnp.maximum(best, score[:, first : first + LANES])
        best = jnp.max(best, axis=1, keepdims=True)
        results.append(
            jnp.concatenate([best[t * groups : (t + 1) * groups] for t in range(slots)], axis=1)
        )
    own_low = member < (member ^ CROSS)
    out_ref[:groups, 0, :] = jnp.where(own_low, results[0], results[1])
    out_ref[groups:, 0, :] = jnp.where(own_low, results[1], results[0])


def nearest_of(place, counts, own, chip, cross, nxt):
    rows, width = own.shape
    groups = counts.shape[0]
    vmem = pl.BlockSpec(memory_space=pltpu.VMEM)
    return pl.pallas_call(
        nearest_kernel,
        out_shape=jax.ShapeDtypeStruct((2 * groups, 1, rows // groups), jnp.float32),
        in_specs=[pl.BlockSpec(memory_space=pltpu.SMEM)] + [vmem] * 5,
        out_specs=vmem,
        compiler_params=pltpu.CompilerParams(vmem_limit_bytes=32 << 20),
        cost_estimate=pl.CostEstimate(
            flops=16 * rows * rows * width, bytes_accessed=10 * rows * width, transcendentals=0
        ),
    )(place, counts, own, chip, cross, nxt)


def make_on_device(clusters, members):
    def trade(array, mask):
        return lax.ppermute(array, "mem", [(m, m ^ mask) for m in range(members)])

    def both_cores(array):
        chips = [[m, m ^ CORE] for m in range(0, members, 2)]
        return lax.all_gather(array, "mem", axis=0, axis_index_groups=chips)

    owners = [c ^ FLIP for c in range(clusters)]
    sends = [[c * members + m for c in owners] for m in range(members)]
    lows = [m for m in range(members) if m < m ^ CROSS]
    returns = [
        [c * members + m for m in (low, low ^ CROSS) for c in owners] for low in lows
    ]

    def on_device(embeddings, counts):
        cluster = lax.axis_index("grp") ^ FLIP
        member = lax.axis_index("mem")
        slot_dev = embeddings.shape[1]
        groups = embeddings.shape[2]
        width = embeddings.shape[3]
        local = embeddings.reshape(slot_dev, groups, width)
        values = local.astype(jnp.float32)
        units = (
            values * lax.rsqrt(jnp.sum(values * values, axis=-1, keepdims=True) + EPS)
        ).astype(jnp.bfloat16)
        owned = lax.all_to_all(
            units, ("grp", "mem"), split_axis=1, concat_axis=1, tiled=True, axis_index_groups=sends
        )
        rows = owned.reshape(slot_dev * groups, width)
        next_rows = trade(rows, NEXT)
        cross_rows = trade(rows, CROSS)
        chip_rows = both_cores(rows)
        next_chip_rows = both_cores(next_rows)
        place = jnp.stack([cluster, member]).astype(jnp.int32)
        best = nearest_of(place, counts, rows, chip_rows, cross_rows, next_chip_rows)
        back = lax.all_to_all(
            best, ("grp", "mem"), split_axis=0, concat_axis=0, tiled=True, axis_index_groups=returns
        )
        back = jnp.max(back.reshape(2, groups, slot_dev), axis=0)
        return back.T.reshape(1, slot_dev, groups)

    return on_device


def solution(mesh):
    return jax.shard_map(
        make_on_device(mesh.shape["grp"], mesh.shape["mem"]),
        mesh=mesh,
        in_specs=(P("grp", "mem", None, None), P()),
        out_specs=P("grp", "mem", None),
        check_vma=False,
    )
```

```python
import jax
import jax.numpy as jnp
from jax import lax
from jax.experimental import pallas as pl
from jax.experimental.pallas import tpu as pltpu
from jax.sharding import PartitionSpec as P

EPS = 1e-06
FAR = 1 << 20
LANES = 128
CORE, NEXT, CROSS = 1, 6, 2
FAR_HALF, NEAR_HALF = 34, 62


def group_at(place, half):
    return place ^ jnp.where(place % (2 * half) < half, FAR_HALF, NEAR_HALF)


def place_of(group, half):
    return group ^ jnp.where(group < half, NEAR_HALF, FAR_HALF)


def nearest_kernel(place_ref, counts_ref, own_ref, chip_ref, cross_ref, next_ref, out_ref):
    cluster, member = place_ref[0], place_ref[1]
    rows = own_ref.shape[0]
    groups = counts_ref.shape[0]
    slots = rows // groups
    column = lax.broadcasted_iota(jnp.int32, counts_ref.shape, 1)
    sizes = jnp.sum(jnp.where(column == cluster, counts_ref[...], 0), axis=1, keepdims=True)
    source = lax.broadcasted_iota(jnp.int32, (groups, groups), 0)
    place = lax.broadcasted_iota(jnp.int32, (groups, groups), 1)
    sizes = jnp.sum(jnp.where(source == group_at(place, groups // 2), sizes, 0), axis=0, keepdims=True)
    sizes = jnp.concatenate([sizes] * slots, axis=1)
    lane = group_at(lax.broadcasted_iota(jnp.int32, (1, rows), 1), groups // 2)
    row = group_at(lax.broadcasted_iota(jnp.int32, (rows, 1), 0), groups // 2)

    keys = []
    for keys_ref, first in ((chip_ref, member & ~CORE), (next_ref, (member ^ NEXT) & ~CORE)):
        for core in range(2):
            start = (first + core) * rows
            slot = (start + lane) // groups
            keys.append((keys_ref, core, jnp.where(slot < sizes, start + lane, FAR)))
    results = []
    for query_ref, mask in ((own_ref, 0), (cross_ref, CROSS)):
        query_pos = (member ^ mask) * rows + row
        best = jnp.full((rows, LANES), -1.0, jnp.float32)
        for keys_ref, core, key_pos in keys:
            score = lax.dot_general(
                query_ref[...], keys_ref[core], (((1,), (1,)), ((), ())), preferred_element_type=jnp.float32
            )
            score = jnp.where(key_pos < query_pos, score, -1.0)
            for first in range(0, rows, LANES):
                best = jnp.maximum(best, score[:, first : first + LANES])
        best = jnp.max(best, axis=1, keepdims=True)
        results.append(
            jnp.concatenate([best[t * groups : (t + 1) * groups] for t in range(slots)], axis=1)
        )
    own_low = member < (member ^ CROSS)
    out_ref[:groups, 0, :] = jnp.where(own_low, results[0], results[1])
    out_ref[groups:, 0, :] = jnp.where(own_low, results[1], results[0])


def nearest_of(place, counts, own, chip, cross, nxt):
    rows, width = own.shape
    groups = counts.shape[0]
    vmem = pl.BlockSpec(memory_space=pltpu.VMEM)
    return pl.pallas_call(
        nearest_kernel,
        out_shape=jax.ShapeDtypeStruct((2 * groups, 1, rows // groups), jnp.float32),
        in_specs=[pl.BlockSpec(memory_space=pltpu.SMEM)] + [vmem] * 5,
        out_specs=vmem,
        compiler_params=pltpu.CompilerParams(vmem_limit_bytes=32 << 20),
        cost_estimate=pl.CostEstimate(
            flops=16 * rows * rows * width, bytes_accessed=10 * rows * width, transcendentals=0
        ),
    )(place, counts, own, chip, cross, nxt)


def make_on_device(clusters, members):
    def trade(array, mask):
        return lax.ppermute(array, "mem", [(m, m ^ mask) for m in range(members)])

    def both_cores(array):
        chips = [[m, m ^ CORE] for m in range(0, members, 2)]
        return lax.all_gather(array, "mem", axis=0, axis_index_groups=chips)

    owners = [c ^ (FAR_HALF if c < clusters // 2 else NEAR_HALF) for c in range(clusters)]
    sends = [[c * members + m for c in owners] for m in range(members)]
    lows = [m for m in range(members) if m < m ^ CROSS]
    returns = [
        [c * members + m for m in (low, low ^ CROSS) for c in owners] for low in lows
    ]

    def on_device(embeddings, counts):
        cluster = place_of(lax.axis_index("grp"), clusters // 2)
        member = lax.axis_index("mem")
        slot_dev = embeddings.shape[1]
        groups = embeddings.shape[2]
        width = embeddings.shape[3]
        local = embeddings.reshape(slot_dev, groups, width)
        values = local.astype(jnp.float32)
        units = (
            values * lax.rsqrt(jnp.sum(values * values, axis=-1, keepdims=True) + EPS)
        ).astype(jnp.bfloat16)
        owned = lax.all_to_all(
            units, ("grp", "mem"), split_axis=1, concat_axis=1, tiled=True, axis_index_groups=sends
        )
        rows = owned.reshape(slot_dev * groups, width)
        next_rows = trade(rows, NEXT)
        cross_rows = trade(rows, CROSS)
        chip_rows = both_cores(rows)
        next_chip_rows = both_cores(next_rows)
        place = jnp.stack([cluster, member]).astype(jnp.int32)
        best = nearest_of(place, counts, rows, chip_rows, cross_rows, next_chip_rows)
        back = lax.all_to_all(
            best, ("grp", "mem"), split_axis=0, concat_axis=0, tiled=True, axis_index_groups=returns
        )
        back = jnp.max(back.reshape(2, groups, slot_dev), axis=0)
        return back.T.reshape(1, slot_dev, groups)

    return on_device


def solution(mesh):
    return jax.shard_map(
        make_on_device(mesh.shape["grp"], mesh.shape["mem"]),
        mesh=mesh,
        in_specs=(P("grp", "mem", None, None), P()),
        out_specs=P("grp", "mem", None),
        check_vma=False,
    )
```

```python
import jax
import jax.numpy as jnp
from jax import lax
from jax.experimental import pallas as pl
from jax.experimental.pallas import tpu as pltpu
from jax.sharding import PartitionSpec as P

EPS = 1e-06
FAR = 1 << 20
LANES = 128
CORE, NEXT, CROSS = 1, 6, 2
PLANES = (8, 4, 12, 7, 9, 3, 13, 6, 10, 2, 14, 5, 11, 1, 15, 0)
LINES = (2, 1, 3, 0)
ORDER = [plane * len(LINES) + line for plane in PLANES for line in LINES]


def group_at(place):
    plane, line = jnp.zeros_like(place), jnp.zeros_like(place)
    for index, value in enumerate(PLANES):
        plane = jnp.where(place // len(LINES) == index, value, plane)
    for index, value in enumerate(LINES):
        line = jnp.where(place % len(LINES) == index, value, line)
    return plane * len(LINES) + line


def nearest_kernel(place_ref, counts_ref, own_ref, chip_ref, cross_ref, next_ref, out_ref):
    group, member = place_ref[0], place_ref[1]
    rows = own_ref.shape[0]
    groups = counts_ref.shape[0]
    slots = rows // groups
    across = group_at(lax.broadcasted_iota(jnp.int32, (1, groups), 1))
    down = group_at(lax.broadcasted_iota(jnp.int32, (groups, 1), 0))
    sizes = jnp.sum(jnp.where(across == group, counts_ref[...], 0), axis=1, keepdims=True)
    source = lax.broadcasted_iota(jnp.int32, (groups, groups), 0)
    sizes = jnp.sum(jnp.where(source == across, sizes, 0), axis=0, keepdims=True)
    sizes = jnp.concatenate([sizes] * slots, axis=1)
    lane = jnp.concatenate([across + t * groups for t in range(slots)], axis=1)
    row = jnp.concatenate([down + t * groups for t in range(slots)], axis=0)

    keys = []
    for keys_ref, first in ((chip_ref, member & ~CORE), (next_ref, (member ^ NEXT) & ~CORE)):
        for core in range(2):
            start = (first + core) * rows
            slot = (start + lane) // groups
            keys.append((keys_ref, core, jnp.where(slot < sizes, start + lane, FAR)))
    results = []
    for query_ref, mask in ((own_ref, 0), (cross_ref, CROSS)):
        query_pos = (member ^ mask) * rows + row
        best = jnp.full((rows, LANES), -1.0, jnp.float32)
        for keys_ref, core, key_pos in keys:
            score = lax.dot_general(
                query_ref[...], keys_ref[core], (((1,), (1,)), ((), ())), preferred_element_type=jnp.float32
            )
            score = jnp.where(key_pos < query_pos, score, -1.0)
            for first in range(0, rows, LANES):
                best = jnp.maximum(best, score[:, first : first + LANES])
        best = jnp.max(best, axis=1, keepdims=True)
        results.append(
            jnp.concatenate([best[t * groups : (t + 1) * groups] for t in range(slots)], axis=1)
        )
    own_low = member < (member ^ CROSS)
    out_ref[:groups, 0, :] = jnp.where(own_low, results[0], results[1])
    out_ref[groups:, 0, :] = jnp.where(own_low, results[1], results[0])


def nearest_of(place, counts, own, chip, cross, nxt):
    rows, width = own.shape
    groups = counts.shape[0]
    vmem = pl.BlockSpec(memory_space=pltpu.VMEM)
    return pl.pallas_call(
        nearest_kernel,
        out_shape=jax.ShapeDtypeStruct((2 * groups, 1, rows // groups), jnp.float32),
        in_specs=[pl.BlockSpec(memory_space=pltpu.SMEM)] + [vmem] * 5,
        out_specs=vmem,
        compiler_params=pltpu.CompilerParams(vmem_limit_bytes=32 << 20),
        cost_estimate=pl.CostEstimate(
            flops=16 * rows * rows * width, bytes_accessed=10 * rows * width, transcendentals=0
        ),
    )(place, counts, own, chip, cross, nxt)


def make_on_device(clusters, members):
    def trade(array, mask):
        return lax.ppermute(array, "mem", [(m, m ^ mask) for m in range(members)])

    def both_cores(array):
        chips = [[m, m ^ CORE] for m in range(0, members, 2)]
        return lax.all_gather(array, "mem", axis=0, axis_index_groups=chips)

    assert sorted(ORDER) == list(range(clusters))
    sends = [[c * members + m for c in ORDER] for m in range(members)]
    lows = [m for m in range(members) if m < m ^ CROSS]
    returns = [[c * members + m for m in (low, low ^ CROSS) for c in ORDER] for low in lows]

    def on_device(embeddings, counts):
        group = lax.axis_index("grp")
        member = lax.axis_index("mem")
        slot_dev = embeddings.shape[1]
        groups = embeddings.shape[2]
        width = embeddings.shape[3]
        local = embeddings.reshape(slot_dev, groups, width)
        values = local.astype(jnp.float32)
        units = (
            values * lax.rsqrt(jnp.sum(values * values, axis=-1, keepdims=True) + EPS)
        ).astype(jnp.bfloat16)
        owned = lax.all_to_all(
            units, ("grp", "mem"), split_axis=1, concat_axis=1, tiled=True, axis_index_groups=sends
        )
        rows = owned.reshape(slot_dev * groups, width)
        next_rows = trade(rows, NEXT)
        cross_rows = trade(rows, CROSS)
        chip_rows = both_cores(rows)
        next_chip_rows = both_cores(next_rows)
        place = jnp.stack([group, member]).astype(jnp.int32)
        best = nearest_of(place, counts, rows, chip_rows, cross_rows, next_chip_rows)
        back = lax.all_to_all(
            best, ("grp", "mem"), split_axis=0, concat_axis=0, tiled=True, axis_index_groups=returns
        )
        back = jnp.max(back.reshape(2, groups, slot_dev), axis=0)
        return back.T.reshape(1, slot_dev, groups)

    return on_device


def solution(mesh):
    return jax.shard_map(
        make_on_device(mesh.shape["grp"], mesh.shape["mem"]),
        mesh=mesh,
        in_specs=(P("grp", "mem", None, None), P()),
        out_specs=P("grp", "mem", None),
        check_vma=False,
    )
```

```python
import jax
import jax.numpy as jnp
from jax import lax
from jax.experimental import pallas as pl
from jax.experimental.pallas import tpu as pltpu
from jax.sharding import PartitionSpec as P

EPS = 1e-06
FAR = 1 << 20
LANES = 128
LOAD = 16
CORE, NEXT, CROSS = 1, 6, 2
PLANES = (8, 4, 12, 7, 9, 3, 13, 6, 10, 2, 14, 5, 11, 1, 15, 0)
LINES = (2, 1, 3, 0)
ORDER = [plane * len(LINES) + line for plane in PLANES for line in LINES]


def group_at(place):
    plane, line = jnp.zeros_like(place), jnp.zeros_like(place)
    for index, value in enumerate(PLANES):
        plane = jnp.where(place // len(LINES) == index, value, plane)
    for index, value in enumerate(LINES):
        line = jnp.where(place % len(LINES) == index, value, line)
    return plane * len(LINES) + line


def unit_kernel(items_ref, units_ref, stage_ref, sems):
    steps, _, rows, _ = stage_ref.shape

    def load(step):
        part = pl.ds(step * rows, rows)
        return pltpu.make_async_copy(items_ref.at[0, :, part], stage_ref.at[step], sems.at[step])

    for step in range(steps):
        load(step).start()
    for step in range(steps):
        load(step).wait()
        values = stage_ref[step].astype(jnp.float32)
        total = jnp.sum(values * values, axis=-1, keepdims=True)
        units = values * lax.rsqrt(total + EPS)
        units_ref[step * rows : (step + 1) * rows] = jnp.transpose(units, (1, 0, 2)).astype(jnp.bfloat16)


def units_by_cluster(embeddings):
    _, slots, clusters, width = embeddings.shape
    size = slots * clusters * width
    return pl.pallas_call(
        unit_kernel,
        out_shape=jax.ShapeDtypeStruct((clusters, slots, width), jnp.bfloat16),
        in_specs=[pl.BlockSpec(memory_space=pltpu.HBM)],
        out_specs=pl.BlockSpec(memory_space=pltpu.VMEM),
        scratch_shapes=[
            pltpu.VMEM((clusters // LOAD, slots, LOAD, width), jnp.bfloat16),
            pltpu.SemaphoreType.DMA((clusters // LOAD,)),
        ],
        compiler_params=pltpu.CompilerParams(vmem_limit_bytes=107 << 19),
        cost_estimate=pl.CostEstimate(
            flops=4 * size, bytes_accessed=4 * size, transcendentals=slots * clusters
        ),
    )(embeddings)


def nearest_kernel(place_ref, counts_ref, own_ref, chip_ref, cross_ref, next_ref, out_ref):
    group, member = place_ref[0], place_ref[1]
    rows = own_ref.shape[0]
    groups = counts_ref.shape[0]
    slots = rows // groups
    across = group_at(lax.broadcasted_iota(jnp.int32, (1, groups), 1))
    down = group_at(lax.broadcasted_iota(jnp.int32, (groups, 1), 0))
    sizes = jnp.sum(jnp.where(across == group, counts_ref[...], 0), axis=1, keepdims=True)
    source = lax.broadcasted_iota(jnp.int32, (groups, groups), 0)
    sizes = jnp.sum(jnp.where(source == across, sizes, 0), axis=0, keepdims=True)
    sizes = jnp.concatenate([sizes] * slots, axis=1)
    lane = jnp.concatenate([across + t * groups for t in range(slots)], axis=1)
    row = jnp.concatenate([down + t * groups for t in range(slots)], axis=0)

    keys = []
    for keys_ref, first in ((chip_ref, member & ~CORE), (next_ref, (member ^ NEXT) & ~CORE)):
        for core in range(2):
            start = (first + core) * rows
            slot = (start + lane) // groups
            keys.append((keys_ref, core, jnp.where(slot < sizes, start + lane, FAR)))
    results = []
    for query_ref, mask in ((own_ref, 0), (cross_ref, CROSS)):
        query_pos = (member ^ mask) * rows + row
        best = jnp.full((rows, LANES), -1.0, jnp.float32)
        for keys_ref, core, key_pos in keys:
            score = lax.dot_general(
                query_ref[...], keys_ref[core], (((1,), (1,)), ((), ())), preferred_element_type=jnp.float32
            )
            score = jnp.where(key_pos < query_pos, score, -1.0)
            for first in range(0, rows, LANES):
                best = jnp.maximum(best, score[:, first : first + LANES])
        best = jnp.max(best, axis=1, keepdims=True)
        results.append(
            jnp.concatenate([best[t * groups : (t + 1) * groups] for t in range(slots)], axis=1)
        )
    own_low = member < (member ^ CROSS)
    low = jnp.where(own_low, results[0], results[1])
    high = jnp.where(own_low, results[1], results[0])
    out_ref[...] = jnp.stack([low, high], axis=1)


def nearest_of(place, counts, own, chip, cross, nxt):
    rows, width = own.shape
    groups = counts.shape[0]
    vmem = pl.BlockSpec(memory_space=pltpu.VMEM)
    return pl.pallas_call(
        nearest_kernel,
        out_shape=jax.ShapeDtypeStruct((groups, 2, rows // groups), jnp.float32),
        in_specs=[pl.BlockSpec(memory_space=pltpu.SMEM)] + [vmem] * 5,
        out_specs=vmem,
        compiler_params=pltpu.CompilerParams(vmem_limit_bytes=32 << 20),
        cost_estimate=pl.CostEstimate(
            flops=16 * rows * rows * width, bytes_accessed=10 * rows * width, transcendentals=0
        ),
    )(place, counts, own, chip, cross, nxt)


def make_on_device(clusters, members):
    def trade(array, mask):
        return lax.ppermute(array, "mem", [(m, m ^ mask) for m in range(members)])

    def both_cores(array):
        chips = [[m, m ^ CORE] for m in range(0, members, 2)]
        return lax.all_gather(array, "mem", axis=0, axis_index_groups=chips)

    assert sorted(ORDER) == list(range(clusters))
    sends = [[c * members + m for c in ORDER] for m in range(members)]
    lows = [m for m in range(members) if m < m ^ CROSS]
    returns = [[c * members + m for c in ORDER for m in (low, low ^ CROSS)] for low in lows]

    def on_device(embeddings, counts):
        group = lax.axis_index("grp")
        member = lax.axis_index("mem")
        slot_dev = embeddings.shape[1]
        groups = embeddings.shape[2]
        width = embeddings.shape[3]
        units = units_by_cluster(embeddings)
        owned = lax.all_to_all(
            units, ("grp", "mem"), split_axis=0, concat_axis=0, tiled=True, axis_index_groups=sends
        )
        rows = jnp.transpose(owned, (1, 0, 2)).reshape(slot_dev * groups, width)
        next_rows = trade(rows, NEXT)
        cross_rows = trade(rows, CROSS)
        chip_rows = both_cores(rows)
        next_chip_rows = both_cores(next_rows)
        place = jnp.stack([group, member]).astype(jnp.int32)
        best = nearest_of(place, counts, rows, chip_rows, cross_rows, next_chip_rows)
        back = lax.all_to_all(
            best.reshape(2 * groups, 1, slot_dev), ("grp", "mem"), split_axis=0, concat_axis=0, tiled=True, axis_index_groups=returns
        )
        back = jnp.max(back.reshape(groups, 2, slot_dev), axis=1)
        return back.T.reshape(1, slot_dev, groups)

    return on_device


def solution(mesh):
    return jax.shard_map(
        make_on_device(mesh.shape["grp"], mesh.shape["mem"]),
        mesh=mesh,
        in_specs=(P("grp", "mem", None, None), P()),
        out_specs=P("grp", "mem", None),
        check_vma=False,
    )
```

```python
import jax
import jax.numpy as jnp
from jax import lax
from jax.experimental import pallas as pl
from jax.experimental.pallas import tpu as pltpu
from jax.sharding import PartitionSpec as P

EPS = 1e-06
FAR = 1 << 20
LANES = 128
LOAD = 16
CORE, NEXT, CROSS = 1, 6, 2
PLANES = (8, 4, 12, 7, 9, 3, 13, 6, 10, 2, 14, 5, 11, 1, 15, 0)
LINES = (2, 1, 3, 0)
ORDER = [plane * len(LINES) + line for plane in PLANES for line in LINES]


def group_at(place):
    plane, line = jnp.zeros_like(place), jnp.zeros_like(place)
    for index, value in enumerate(PLANES):
        plane = jnp.where(place // len(LINES) == index, value, plane)
    for index, value in enumerate(LINES):
        line = jnp.where(place % len(LINES) == index, value, line)
    return plane * len(LINES) + line


def unit_kernel(items_ref, units_ref, stage_ref, sems):
    steps, _, rows, _ = stage_ref.shape

    def load(step):
        part = pl.ds(step * rows, rows)
        return pltpu.make_async_copy(items_ref.at[0, :, part], stage_ref.at[step], sems.at[step])

    for step in range(steps):
        load(step).start()
    for step in range(steps):
        load(step).wait()
        values = stage_ref[step].astype(jnp.float32)
        total = jnp.sum(values * values, axis=-1, keepdims=True)
        units = values * lax.rsqrt(total + EPS)
        units_ref[step * rows : (step + 1) * rows] = jnp.transpose(units, (1, 0, 2)).astype(jnp.bfloat16)


def units_by_cluster(embeddings):
    _, slots, clusters, width = embeddings.shape
    size = slots * clusters * width
    return pl.pallas_call(
        unit_kernel,
        out_shape=jax.ShapeDtypeStruct((clusters, slots, width), jnp.bfloat16),
        in_specs=[pl.BlockSpec(memory_space=pltpu.HBM)],
        out_specs=pl.BlockSpec(memory_space=pltpu.VMEM),
        scratch_shapes=[
            pltpu.VMEM((clusters // LOAD, slots, LOAD, width), jnp.bfloat16),
            pltpu.SemaphoreType.DMA((clusters // LOAD,)),
        ],
        compiler_params=pltpu.CompilerParams(vmem_limit_bytes=107 << 19),
        cost_estimate=pl.CostEstimate(
            flops=4 * size, bytes_accessed=4 * size, transcendentals=slots * clusters
        ),
    )(embeddings)


def nearest_kernel(place_ref, counts_ref, own_ref, chip_ref, cross_ref, next_ref, out_ref):
    group, member = place_ref[0], place_ref[1]
    rows = own_ref.shape[0]
    groups = counts_ref.shape[0]
    slots = rows // groups
    across = group_at(lax.broadcasted_iota(jnp.int32, (1, groups), 1))
    down = group_at(lax.broadcasted_iota(jnp.int32, (groups, 1), 0))
    sizes = jnp.sum(jnp.where(across == group, counts_ref[...], 0), axis=1, keepdims=True)
    source = lax.broadcasted_iota(jnp.int32, (groups, groups), 0)
    sizes = jnp.sum(jnp.where(source == across, sizes, 0), axis=0, keepdims=True)
    sizes = jnp.concatenate([sizes] * slots, axis=1)
    lane = jnp.concatenate([across + t * groups for t in range(slots)], axis=1)
    row = jnp.concatenate([down + t * groups for t in range(slots)], axis=0)

    keys = []
    for keys_ref, first in ((chip_ref, member & ~CORE), (next_ref, (member ^ NEXT) & ~CORE)):
        places = []
        for core in range(2):
            start = (first + core) * rows
            slot = (start + lane) // groups
            places.append(jnp.where(slot < sizes, start + lane, FAR))
        keys.append((keys_ref, jnp.concatenate(places, axis=1)))
    results = []
    for query_ref, mask in ((own_ref, 0), (cross_ref, CROSS)):
        query_pos = (member ^ mask) * rows + row
        best = jnp.full((rows, LANES), -1.0, jnp.float32)
        for keys_ref, key_pos in keys:
            score = lax.dot_general(
                query_ref[...], keys_ref[...].reshape(2 * rows, -1), (((1,), (1,)), ((), ())), preferred_element_type=jnp.float32
            )
            score = jnp.where(key_pos < query_pos, score, -1.0)
            for first in range(0, 2 * rows, LANES):
                best = jnp.maximum(best, score[:, first : first + LANES])
        best = jnp.max(best, axis=1, keepdims=True)
        results.append(
            jnp.concatenate([best[t * groups : (t + 1) * groups] for t in range(slots)], axis=1)
        )
    own_low = member < (member ^ CROSS)
    low = jnp.where(own_low, results[0], results[1])
    high = jnp.where(own_low, results[1], results[0])
    out_ref[...] = jnp.stack([low, high], axis=1)


def nearest_of(place, counts, own, chip, cross, nxt):
    rows, width = own.shape
    groups = counts.shape[0]
    vmem = pl.BlockSpec(memory_space=pltpu.VMEM)
    return pl.pallas_call(
        nearest_kernel,
        out_shape=jax.ShapeDtypeStruct((groups, 2, rows // groups), jnp.float32),
        in_specs=[pl.BlockSpec(memory_space=pltpu.SMEM)] + [vmem] * 5,
        out_specs=vmem,
        compiler_params=pltpu.CompilerParams(vmem_limit_bytes=32 << 20),
        cost_estimate=pl.CostEstimate(
            flops=16 * rows * rows * width, bytes_accessed=10 * rows * width, transcendentals=0
        ),
    )(place, counts, own, chip, cross, nxt)


def make_on_device(clusters, members):
    def trade(array, mask):
        return lax.ppermute(array, "mem", [(m, m ^ mask) for m in range(members)])

    def both_cores(array):
        chips = [[m, m ^ CORE] for m in range(0, members, 2)]
        return lax.all_gather(array, "mem", axis=0, axis_index_groups=chips)

    assert sorted(ORDER) == list(range(clusters))
    sends = [[c * members + m for c in ORDER] for m in range(members)]
    lows = [m for m in range(members) if m < m ^ CROSS]
    returns = [[c * members + m for c in ORDER for m in (low, low ^ CROSS)] for low in lows]

    def on_device(embeddings, counts):
        group = lax.axis_index("grp")
        member = lax.axis_index("mem")
        slot_dev = embeddings.shape[1]
        groups = embeddings.shape[2]
        width = embeddings.shape[3]
        units = units_by_cluster(embeddings)
        owned = lax.all_to_all(
            units, ("grp", "mem"), split_axis=0, concat_axis=0, tiled=True, axis_index_groups=sends
        )
        rows = jnp.transpose(owned, (1, 0, 2)).reshape(slot_dev * groups, width)
        next_rows = trade(rows, NEXT)
        cross_rows = trade(rows, CROSS)
        chip_rows = both_cores(rows)
        next_chip_rows = both_cores(next_rows)
        place = jnp.stack([group, member]).astype(jnp.int32)
        best = nearest_of(place, counts, rows, chip_rows, cross_rows, next_chip_rows)
        back = lax.all_to_all(
            best.reshape(2 * groups, 1, slot_dev), ("grp", "mem"), split_axis=0, concat_axis=0, tiled=True, axis_index_groups=returns
        )
        back = jnp.max(back.reshape(groups, 2, slot_dev), axis=1)
        return back.T.reshape(1, slot_dev, groups)

    return on_device


def solution(mesh):
    return jax.shard_map(
        make_on_device(mesh.shape["grp"], mesh.shape["mem"]),
        mesh=mesh,
        in_specs=(P("grp", "mem", None, None), P()),
        out_specs=P("grp", "mem", None),
        check_vma=False,
    )
```
